128 devices in a mesh: region: 64 (over z, y, x_hi, core), obs: 2 (over x_lo).
Axes of the slice: x: 4 (x_hi: 2, x_lo: 2; x = x_hi * 2 + x_lo), y: 4, z: 4, core: 2. Of those that a mesh axis runs over, the one named last changes fastest.
Arguments:
- obs_anomaly: bfloat16 [2048, 2048, 128], P('region', 'obs'), may hold values from -1.5 to 1.5
- innovation: bfloat16 [2048, 2048], P('region', 'obs'), may hold values from -6 to 6
- obs_count: int32 [2048], P('region'), may hold values from 512 to 2048, as said below
- neighbour: int32 [2048, 5], P('region'), may hold values from 0 to 2047, as said below
- taper: float32 [2048, 5], P('region'), may hold values from 0.1 to 1
- param_anomaly: bfloat16 [2048, 1024, 128], P('region', 'obs'), may hold values from -6 to 6
- param_mean: float32 [2048, 1024], P('region', 'obs'), may hold values from -6 to 6
Outputs:
- analysis: bfloat16 [2048, 1024, 128], P('region', 'obs')
The draws below stay inside these ranges and needn't reach their ends.
Inputs may be any that keep to these rules, and one draw needn't show every extreme that they name: `obs_count`: region 2048 counts: some region has all 2048 slots live. neighbour[g, 0] = g; every other entry differs from g cyclically by 1 to 32 regions.
All inputs are finite; a program needn't handle non-finite values.
Results may differ from the reference program's by a relative error of at most 0.013.
Values may be sent and summed in bfloat16 or wider, within the bound.
No kernel may reach another device: no remote copies, remote signals or barrier semaphores. Data moves between devices by JAX's collectives and lax.ppermute only.
A program may use at most 192 MiB of HBM per device.

```python
import jax
import jax.numpy as jnp
from jax import lax

MEMBERS = 128
NB = 5
R_DEV = 32
OBS_REG = 2048
PAR_REG = 1024
NREG = 2048
N_REGION = 64


def draw_obs_anomaly(key, part):
    key = jax.random.fold_in(key, 37)
    key_noise, key_dir, key_coef = jax.random.split(key, 3)
    noise = jax.random.truncated_normal(key_noise, -4.0, 4.0, (NREG, OBS_REG, MEMBERS), jnp.float32)
    direction = jax.random.truncated_normal(key_dir, -2.5, 2.5, (NREG, 1, MEMBERS), jnp.float32)
    amplitude = 0.1
    coefs = jax.random.truncated_normal(key_coef, -2.5, 2.5, (NREG, OBS_REG, 1), jnp.float32)
    values = 0.2 * noise + amplitude * coefs * direction
    return values.astype(jnp.bfloat16)


def draw_obs_count(key, part):
    key = jax.random.fold_in(key, 11)
    key_one, key_two, key_three = jax.random.split(key, 3)
    first = jax.random.randint(key_one, (NREG,), OBS_REG // 4, OBS_REG + 1)
    second = jax.random.randint(key_two, (NREG,), OBS_REG // 4, OBS_REG + 1)
    counts = jnp.minimum(first, second)
    target = jax.random.randint(key_three, (), 0, NREG)
    counts = jnp.where(jnp.arange(NREG) == target, OBS_REG, counts)
    return counts.astype(jnp.int32)


def draw_neighbour(key, part):
    key = jax.random.fold_in(key, 23)
    offsets = jax.random.randint(key, (NREG, NB - 1), 1, R_DEV + 1)
    signs = jnp.where(jnp.arange(NB - 1) % 2 == 0, 1, -1)
    own = jnp.arange(NREG, dtype=jnp.int32)
    others = (own[:, None] + signs[None, :] * offsets) % NREG
    return jnp.concatenate([own[:, None], others], axis=1).astype(jnp.int32)


def levels(stream_key, shape, pieces, low, high):
    loudness, own = 1.0, jax.random.fold_in(stream_key, 6)
    for position, parts in pieces:
        draws = jnp.exp(jax.random.uniform(jax.random.fold_in(own, position), (parts,), jnp.float32, low / len(pieces), high / len(pieces)))
        loudness = loudness * jnp.repeat(draws, shape[position] // parts).reshape([-1 if axis == position else 1 for axis in range(len(shape))])
    return loudness


def gaussian(rng, extent, scale, reach, shards=(), held_as=jnp.bfloat16):
    result = scale * jax.random.normal(rng, extent, jnp.float32)
    if shards:
        result = result * levels(rng, extent, shards, -0.22, 0.18)
    return jnp.clip(result, -reach, reach).astype(held_as)


def setup_inputs(seed: int = 0) -> dict:
    key_of = jax.random.split(jax.random.key(seed), 8)
    return {
        "obs_anomaly": draw_obs_anomaly(jax.random.fold_in(key_of[7], 71), 0),
        "innovation": gaussian(key_of[1], (NREG, OBS_REG), 1.0, 6.0, ((0, 64), (1, 2))),
        "obs_count": draw_obs_count(jax.random.fold_in(key_of[7], 71), 0),
        "neighbour": draw_neighbour(jax.random.fold_in(key_of[7], 71), 0),
        "taper": jnp.clip(0.1 + 0.9 * jax.random.uniform(key_of[4], (NREG, NB), jnp.float32) ** levels(key_of[4], (NREG, NB), ((0, 64),), -0.2, 0.2), 0.1, 1.0),
        "param_anomaly": gaussian(key_of[5], (NREG, PAR_REG, MEMBERS), 1.0, 6.0, ((0, 64), (1, 2))),
        "param_mean": gaussian(key_of[6], (NREG, PAR_REG), 1.0, 6.0, ((0, 64), (1, 2)), jnp.float32),
    }


def lower_inverse(lower):
    width = lower.shape[-1]
    rows = jnp.arange(width, dtype=jnp.int32)[:, None]
    cols = jnp.arange(width, dtype=jnp.int32)[None, :]
    diag = jnp.diagonal(lower, axis1=-2, axis2=-1)
    inverse = jnp.where(rows == cols, (1.0 / diag)[..., None, :], jnp.zeros((), jnp.float32))
    block = 1
    while block < width:
        row_block = rows // block
        col_block = cols // block
        keep = (row_block % 2 == 1) & (col_block == row_block - 1)
        corner = jnp.where(keep, lower, jnp.zeros((), jnp.float32))
        inner = jnp.einsum('bij,bjk->bik', corner, inverse, precision=lax.Precision.HIGHEST)
        inverse = inverse - jnp.einsum('bij,bjk->bik', inverse, inner, precision=lax.Precision.HIGHEST)
        block = block * 2
    return inverse

def solve_region(local_gram, local_proj):
    width = local_gram.shape[-1]
    eye = jnp.eye(width, dtype=jnp.float32)
    precision_mat = (width - 1.0) * eye + local_gram
    lower = jnp.linalg.cholesky(precision_mat)
    inverse_lower = lower_inverse(lower)
    step_one = jnp.einsum('bij,bj->bi', inverse_lower, local_proj, precision=lax.Precision.HIGHEST)
    mean_weight = jnp.einsum('bji,bj->bi', inverse_lower, step_one, precision=lax.Precision.HIGHEST)
    spread = jnp.sqrt(width - 1.0) * jnp.swapaxes(inverse_lower, -1, -2)
    return (mean_weight[..., None] + spread).astype(jnp.bfloat16)

def reference(obs_anomaly, innovation, obs_count, neighbour, taper, param_anomaly, param_mean):
    slots = jnp.arange(OBS_REG, dtype=jnp.int32)
    live = slots[None, :] < obs_count[:, None]
    masked_y = jnp.where(live[..., None], obs_anomaly, jnp.zeros((), jnp.bfloat16))
    masked_d = jnp.where(live, innovation, jnp.zeros((), jnp.bfloat16))
    blocks_y = masked_y.reshape(N_REGION, R_DEV, OBS_REG, MEMBERS)
    blocks_d = masked_d.reshape(N_REGION, R_DEV, OBS_REG)

    def grams_of(pair):
        ys, ds = pair
        yf = ys.astype(jnp.float32)
        gram = jnp.einsum('roi,roj->rij', yf, yf, precision=lax.Precision.HIGHEST)
        proj = jnp.einsum('roi,ro->ri', yf, ds.astype(jnp.float32), precision=lax.Precision.HIGHEST)
        return (gram, proj)
    gram, proj = lax.map(grams_of, (blocks_y, blocks_d))
    gram = gram.reshape(NREG, MEMBERS, MEMBERS)
    proj = proj.reshape(NREG, MEMBERS)

    def combine(pair):
        idx, wts = pair
        local_gram = jnp.einsum('rk,rkij->rij', wts, gram[idx], precision=lax.Precision.HIGHEST)
        local_proj = jnp.einsum('rk,rki->ri', wts, proj[idx], precision=lax.Precision.HIGHEST)
        return solve_region(local_gram, local_proj)
    transform = lax.map(combine, (neighbour.reshape(N_REGION, R_DEV, NB), taper.reshape(N_REGION, R_DEV, NB)))
    transform = transform.reshape(NREG, MEMBERS, MEMBERS)
    moved = jnp.einsum('rpk,rkj->rpj', param_anomaly.astype(jnp.float32), transform.astype(jnp.float32), precision=lax.Precision.HIGHEST)
    return (param_mean[..., None] + moved).astype(jnp.bfloat16)
```

```python
import functools

import jax
import jax.numpy as jnp
from jax import lax
from jax.experimental import pallas as pl
from jax.experimental.pallas import tpu as pltpu
from jax.sharding import PartitionSpec as P

N = 128
HALF = 64
BLK = 16
GRP = 16
F32 = jnp.float32
BF16 = jnp.bfloat16


def iota(shape, dim):
    return lax.broadcasted_iota(jnp.int32, shape, dim)


def pack(gram):
    top, bottom = gram[:HALF], pltpu.roll(gram[HALF:], HALF, 1)
    return jnp.where(iota((HALF, N), 1) >= iota((HALF, N), 0), top, bottom)


def gram_kernel(step, count_ref, y_ref, d_ref, out_ref):
    slots = y_ref.shape[1]
    base = pl.program_id(0) * step
    total = d_ref.shape[0]
    rows = lax.broadcasted_iota(jnp.int16, (slots, N), 0)
    drows = iota((BLK, N), 0)
    for s in range(step):
        r = base + s
        live = jnp.clip(count_ref[r], 0, slots).astype(jnp.int16)
        y = jnp.where(rows < live, y_ref[s], jnp.zeros((), BF16))
        start = pl.multiple_of((r // BLK) * BLK, BLK)
        lhs = jnp.concatenate([y.T, d_ref[pl.ds(start, BLK), :]], axis=0)
        full = jnp.dot(lhs, y, preferred_element_type=F32)
        gram = full[:N]
        proj = jnp.sum(jnp.where(drows == r - start, full[N:], 0.0), axis=0, keepdims=True)
        diag = jnp.sum(
            jnp.where(iota((HALF, N), 0) + HALF == iota((HALF, N), 1), gram[HALF:], 0.0),
            axis=0, keepdims=True,
        )
        out_ref[r] = pack(gram).astype(BF16)
        at = iota((total, N), 0) == r
        extra_d, extra_p = out_ref[total, 0:total], out_ref[total, total:2 * total]
        out_ref[total, 0:total] = jnp.where(at, diag, extra_d.astype(F32)).astype(BF16)
        out_ref[total, total:2 * total] = jnp.where(at, proj, extra_p.astype(F32)).astype(BF16)


def grams(live, obs_anomaly, innovation, step=4):
    regions, slots, _ = obs_anomaly.shape
    return pl.pallas_call(
        functools.partial(gram_kernel, step),
        out_shape=jax.ShapeDtypeStruct((regions + 1, HALF, N), BF16),
        grid_spec=pltpu.PrefetchScalarGridSpec(
            num_scalar_prefetch=1,
            grid=(regions // step,),
            in_specs=[
                pl.BlockSpec((step, slots, N), lambda i, c: (i, 0, 0)),
                pl.BlockSpec((regions, slots), lambda i, c: (0, 0)),
            ],
            out_specs=pl.BlockSpec((regions + 1, HALF, N), lambda i, c: (0, 0, 0)),
        ),
        compiler_params=pltpu.CompilerParams(vmem_limit_bytes=48 << 20),
        name="grams",
    )(live, obs_anomaly, innovation)


def split(x):
    high = x.astype(BF16)
    return high, (x - high.astype(F32)).astype(BF16)


def expand(pair_packed, diags, mat_ref, row_a, row_b):
    la, lb = pair_packed
    i, j = iota((HALF, N), 0), iota((HALF, N), 1)
    turned = jnp.concatenate([la, lb], axis=0).T
    top, bottom = turned[:HALF], turned[HALF:]
    top_r, bottom_r = pltpu.roll(top, HALF, 1), pltpu.roll(bottom, HALF, 1)
    ridge = jnp.where(i == j, N - 1.0, 0.0)
    for row, lp, tt, tl, tr, dg in (
        (row_a, la, top, bottom, top_r, diags[0]), (row_b, lb, top_r, bottom_r, top, diags[1]),
    ):
        mat_ref[pl.ds(row, HALF), :] = jnp.where(i <= j, lp, tt) + ridge
        corner = jnp.where(i + HALF > j, pltpu.roll(lp, HALF, 1), tr)
        corner = jnp.where(i + HALF == j, dg + (N - 1.0), corner)
        mat_ref[pl.ds(row + HALF, HALF), :] = jnp.where(j < HALF, tl, corner)


def panel(mat_ref, z_ref, proj, mean, first, kb, last):
    lane = iota((GRP, N), 1)
    rows = [mat_ref[pl.ds(first * N + kb + i, GRP, stride=N), :] for i in range(BLK)]
    done = []
    for i in range(BLK):
        c = kb + i
        pivot = rows[i][:, c:c + 1]
        scale = lax.rsqrt(pivot)
        r = jnp.where(lane == c, 1.0, rows[i]) * scale
        done.append(jnp.where((lane > c) & (lane < kb + BLK), 0.0, r))
        for j in range(i + 1, BLK):
            factor = rows[i][:, kb + j:kb + j + 1] * scale
            rows[j] = jnp.where(lane == c, 0.0, rows[j]) - factor * r
        w = jnp.where(lane <= c, r, 0.0)
        mat_ref[pl.ds(first * N + c, GRP, stride=N), :] = w
        mean = mean + jnp.sum(w * proj, axis=1, keepdims=True) * w
    if not last:
        for j in range(BLK):
            z = done[j][:, kb + j:kb + j + 1] * done[j]
            for i in range(j + 1, BLK):
                z = z + done[i][:, kb + j:kb + j + 1] * done[i]
            z_ref[pl.ds(first * BLK + j, GRP, stride=BLK), :] = z
    return mean


def update(mat_ref, z_ref, m, kb):
    n = N - kb - BLK
    start = pl.multiple_of(m * N + kb + BLK, BLK)
    mat = mat_ref[pl.ds(start, n), :]
    high, low = split(mat)
    zh, zl = split(z_ref[pl.ds(pl.multiple_of(m * BLK, BLK), BLK), :])
    above, below = jnp.zeros((kb, N), BF16), jnp.zeros((n, N), BF16)

    def place(z):
        return jnp.concatenate([p for p in (above, z, below) if p.shape[0]], axis=0)

    bh, bl = place(zh), place(zl)
    change = jnp.dot(
        jnp.concatenate([high, low], axis=1), jnp.concatenate([bh, bh], axis=0),
        preferred_element_type=F32,
    ) + jnp.dot(high, bl, preferred_element_type=F32)
    lane = iota((n, N), 1)
    kept = jnp.where((lane >= kb) & (lane < kb + BLK), 0.0, mat)
    mat_ref[pl.ds(start, n), :] = kept - change


def solve_kernel(idx_ref, taper_ref, idxv_ref, taperv_ref, own_ref, near_ref, far_ref, out_ref,
                 wide_ref, mat_ref, z_ref, diag_ref, mean_ref, sems):
    regions = idxv_ref.shape[0]
    nb = idxv_ref.shape[1]
    copies = [
        pltpu.make_async_copy(src.at[pl.ds(0, regions)], wide_ref.at[pl.ds(s * regions, regions)], sems.at[s])
        for s, src in enumerate((own_ref, near_ref, far_ref))
    ] + [
        pltpu.make_async_copy(src.at[regions], wide_ref.at[3 * regions + s], sems.at[3 + s])
        for s, src in enumerate((own_ref, near_ref, far_ref))
    ]
    for c in copies:
        c.start()
    for c in copies:
        c.wait()
    tails = [wide_ref[3 * regions + s].astype(F32) for s in range(3)]
    sel_lane = iota((regions, 3 * regions), 1)
    weights = jnp.zeros((regions, 3 * regions), F32)
    for k in range(nb):
        weights = weights + jnp.where(sel_lane == idxv_ref[:, k:k + 1], taperv_ref[:, k:k + 1], 0.0)
    diag_all = jnp.concatenate([t[:regions] for t in tails], axis=0)
    proj_all = jnp.concatenate([t[regions:2 * regions] for t in tails], axis=0)
    diag_ref[...] = jnp.dot(weights, diag_all, precision=lax.Precision.HIGHEST, preferred_element_type=F32)
    proj = jnp.dot(weights, proj_all, precision=lax.Precision.HIGHEST, preferred_element_type=F32)

    def combine(pair, _):
        packed = []
        for q in range(2):
            r = 2 * pair + q
            acc = None
            for k in range(nb):
                term = taper_ref[r * nb + k] * wide_ref[idx_ref[r * nb + k]].astype(F32)
                acc = term if acc is None else acc + term
            packed.append(acc)
        row = pl.multiple_of(2 * pair * N, N)
        expand(packed, [diag_ref[pl.ds(2 * pair + q, 1), :] for q in range(2)], mat_ref, row, row + N)
        return 0

    lax.fori_loop(0, regions // 2, combine, 0)
    groups = regions // GRP
    means = [jnp.zeros((GRP, N), F32) for _ in range(groups)]
    for kb in range(0, N, BLK):
        last = kb + BLK == N
        for g in range(groups):
            means[g] = panel(mat_ref, z_ref, proj[g * GRP:(g + 1) * GRP], means[g], g * GRP, kb, last)
        if not last:
            def many(t, _):
                for u in range(8):
                    update(mat_ref, z_ref, t * 8 + u, kb)
                return 0

            lax.fori_loop(0, regions // 8, many, 0)
    mean_ref[...] = jnp.concatenate(means, axis=0)

    def finish(m, _):
        w = mat_ref[pl.ds(pl.multiple_of(m * N, N), N), :]
        out_ref[m] = (jnp.sqrt(jnp.float32(N - 1)) * w + mean_ref[pl.ds(m, 1), :]).astype(BF16)
        return 0

    lax.fori_loop(0, regions, finish, 0, unroll=2)


def solve(idx, taper, own, near, far):
    regions, nb = idx.shape
    hbm = pl.BlockSpec(memory_space=pl.ANY)
    smem = pl.BlockSpec(memory_space=pltpu.SMEM)
    vmem = pl.BlockSpec(memory_space=pltpu.VMEM)
    return pl.pallas_call(
        solve_kernel,
        out_shape=jax.ShapeDtypeStruct((regions, N, N), BF16),
        in_specs=[smem, smem, vmem, vmem, hbm, hbm, hbm],
        out_specs=vmem,
        scratch_shapes=[
            pltpu.VMEM((3 * regions + 3, HALF, N), BF16),
            pltpu.VMEM((regions * N, N), F32),
            pltpu.VMEM((regions * BLK, N), F32),
            pltpu.VMEM((regions, N), F32),
            pltpu.VMEM((regions, N), F32),
            pltpu.SemaphoreType.DMA((6,)),
        ],
        compiler_params=pltpu.CompilerParams(vmem_limit_bytes=48 << 20),
        name="solve",
    )(idx.reshape(-1), taper.reshape(-1), idx, taper, own, near, far)


def apply_kernel(step, mean_ref, turned_ref, param_ref, out_ref, column_ref):
    regions = mean_ref.shape[0]

    @pl.when(pl.program_id(0) == 0)
    def _():
        rest = mean_ref[...]
        pieces = []
        for _ in range(3):
            high = rest.astype(BF16).astype(F32)
            pieces.append(high)
            rest = rest - high
        pieces.append(jnp.zeros((N - 3 * regions, rest.shape[1]), F32))
        column_ref[...] = jnp.concatenate(pieces, axis=0).T.astype(BF16)

    lane = iota((N, N), 1)
    for s in range(step):
        r = pl.program_id(0) * step + s
        pick = ((lane == r) | (lane == regions + r) | (lane == 2 * regions + r)).astype(F32).astype(BF16)
        left = jnp.concatenate([param_ref[s], column_ref[...]], axis=1)
        right = jnp.concatenate([turned_ref[s], pick], axis=1)
        moved = lax.dot_general(left, right, (((1,), (1,)), ((), ())), preferred_element_type=F32)
        out_ref[s] = moved.astype(BF16)


def apply(param_mean, turned, param_anomaly, step=4):
    regions, params, _ = param_anomaly.shape
    return pl.pallas_call(
        functools.partial(apply_kernel, step),
        out_shape=jax.ShapeDtypeStruct(param_anomaly.shape, BF16),
        grid=(regions // step,),
        in_specs=[
            pl.BlockSpec((regions, params), lambda i: (0, 0)),
            pl.BlockSpec((step, N, N), lambda i: (i, 0, 0)),
            pl.BlockSpec((step, params, N), lambda i: (i, 0, 0)),
        ],
        out_specs=pl.BlockSpec((step, params, N), lambda i: (i, 0, 0)),
        scratch_shapes=[pltpu.VMEM((params, N), BF16)],
        compiler_params=pltpu.CompilerParams(vmem_limit_bytes=48 << 20),
        name="apply",
    )(param_mean, turned, param_anomaly)


def body(obs_anomaly, innovation, obs_count, neighbour, taper, param_anomaly, param_mean):
    regions, slots = obs_anomaly.shape[:2]
    size, half = lax.axis_size("region"), lax.axis_size("obs")
    total = regions * size
    here, part = lax.axis_index("region"), lax.axis_index("obs")
    devices = [(r, o) for r in range(size) for o in range(half)]

    def swap(x, other):
        line = [(r * half + o, (lambda a: (a[0] % size) * half + a[1])(other(r, o))) for r, o in devices]
        return lax.ppermute(x, ("region", "obs"), line)

    packed = grams(obs_count - part * slots, obs_anomaly, innovation)
    partner = swap(packed, lambda r, o: (r, 1 - o))
    own = (packed.astype(F32) + partner.astype(F32)).astype(BF16)
    far = swap(own, lambda r, o: (r + 1 if r % 2 else r - 1, 1 - o))
    near = swap(own, lambda r, o: (r ^ 1, o))
    place = (neighbour - here * regions + regions) % total
    even = here % 2 == 0
    before, after = jnp.where(even, 2, 1), jnp.where(even, 1, 2)
    slot = jnp.where(place < regions, before, jnp.where(place < 2 * regions, 0, after))
    idx = (slot * regions + place % regions).astype(jnp.int32)
    turned = solve(idx, taper, own, near, far)
    return apply(param_mean, turned, param_anomaly)


def solution(mesh):
    specs = (
        P("region", "obs", None), P("region", "obs"), P("region"), P("region", None),
        P("region", None), P("region", "obs", None), P("region", "obs"),
    )
    return jax.shard_map(body, mesh=mesh, in_specs=specs, out_specs=P("region", "obs", None), check_vma=False)
```

```python
import functools

import jax
import jax.numpy as jnp
from jax import lax
from jax.experimental import pallas as pl
from jax.experimental.pallas import tpu as pltpu
from jax.sharding import PartitionSpec as P

N = 128
HALF = 64
CHUNK = 16
BLK = 16
U1, U2, U3 = 32, 16, 4
F32 = jnp.float32
BF16 = jnp.bfloat16


def iota(shape, dim):
    return lax.broadcasted_iota(jnp.int32, shape, dim)


def pack(gram):
    top, bottom = gram[:HALF], pltpu.roll(gram[HALF:], HALF, 1)
    return jnp.where(iota((HALF, N), 1) >= iota((HALF, N), 0), top, bottom)


def gram_kernel(step, first, count_ref, y_ref, d_ref, out_ref, diag_ref, proj_ref):
    slots = y_ref.shape[1]
    total = diag_ref.shape[0]
    base = pl.program_id(0) * step
    rows = lax.broadcasted_iota(jnp.int16, (slots, N), 0)
    on_ridge = iota((HALF, N), 0) + HALF == iota((HALF, N), 1)
    start = pl.multiple_of((base // BLK) * BLK, BLK)
    drows = iota((BLK, N), 0)
    d = d_ref[pl.ds(pl.multiple_of(first + start, BLK), BLK), :]
    for s in range(step):
        r = base + s
        live = jnp.clip(count_ref[first + r], 0, slots).astype(jnp.int16)
        y = jnp.where(rows < live, y_ref[s], jnp.zeros((), BF16))
        full = jnp.dot(jnp.concatenate([y.T, d], axis=0), y, preferred_element_type=F32)
        packed = pack(full[:N]).astype(BF16)
        out_ref[2 * r] = packed[:HALF // 2]
        out_ref[2 * r + 1] = packed[HALF // 2:]
        diag_ref[pl.ds(r, 1), :] = jnp.sum(jnp.where(on_ridge, full[HALF:N], 0.0), axis=0, keepdims=True)
        proj_ref[pl.ds(r, 1), :] = jnp.sum(jnp.where(drows == r - start, full[N:], 0.0), axis=0, keepdims=True)

    @pl.when(pl.program_id(0) == pl.num_programs(0) - 1)
    def _():
        out_ref[2 * total] = jnp.concatenate([diag_ref[...], proj_ref[...]], axis=0).astype(BF16)


def grams(live, obs_anomaly, innovation, first, step=8):
    regions, slots, _ = obs_anomaly.shape
    return pl.pallas_call(
        functools.partial(gram_kernel, step, first),
        out_shape=jax.ShapeDtypeStruct((2 * CHUNK + 1, HALF // 2, N), BF16),
        grid_spec=pltpu.PrefetchScalarGridSpec(
            num_scalar_prefetch=1,
            grid=(CHUNK // step,),
            in_specs=[
                pl.BlockSpec((step, slots, N), lambda i, c: (i + first // step, 0, 0)),
                pl.BlockSpec((regions, slots), lambda i, c: (0, 0)),
            ],
            out_specs=pl.BlockSpec((2 * CHUNK + 1, HALF // 2, N), lambda i, c: (0, 0, 0)),
            scratch_shapes=[pltpu.VMEM((CHUNK, N), F32), pltpu.VMEM((CHUNK, N), F32)],
        ),
        compiler_params=pltpu.CompilerParams(vmem_limit_bytes=48 << 20),
        name="grams",
    )(live, obs_anomaly, innovation)


def split(x):
    high = x.astype(BF16)
    return high, (x - high.astype(F32)).astype(BF16)


def expand(pair_packed, diags, mat_ref, row_a, row_b):
    la, lb = pair_packed
    i, j = iota((HALF, N), 0), iota((HALF, N), 1)
    turned = jnp.concatenate([la, lb], axis=0).T
    top, bottom = turned[:HALF], turned[HALF:]
    top_r, bottom_r = pltpu.roll(top, HALF, 1), pltpu.roll(bottom, HALF, 1)
    ridge = jnp.where(i == j, N - 1.0, 0.0)
    for row, lp, tt, tl, tr, dg in (
        (row_a, la, top, bottom, top_r, diags[0]), (row_b, lb, top_r, bottom_r, top, diags[1]),
    ):
        mat_ref[pl.ds(row, HALF), :] = jnp.where(i <= j, lp, tt) + ridge
        corner = jnp.where(i + HALF > j, pltpu.roll(lp, HALF, 1), tr)
        corner = jnp.where(i + HALF == j, dg + (N - 1.0), corner)
        mat_ref[pl.ds(row + HALF, HALF), :] = jnp.where(j < HALF, tl, corner)


def factor(mat_ref, small_ref, regions, kb):
    sub = iota((BLK, regions), 0)
    x = []
    for i in range(BLK):
        row = mat_ref[pl.ds(kb + i, regions, stride=N), :]
        x.append(row.T[kb:kb + BLK])
    lower = []
    for i in range(BLK):
        scale = lax.rsqrt(x[i][i:i + 1])
        r = jnp.where(sub == i, 1.0, x[i]) * scale
        for j in range(i + 1, BLK):
            x[j] = jnp.where(sub == i, 0.0, x[j]) - (x[i][j:j + 1] * scale) * r
        lower.append(jnp.where(sub <= i, r, 0.0))
    inverse = []
    for a in range(BLK):
        z = lower[a][a:a + 1] * lower[a]
        for i in range(a + 1, BLK):
            z = z + lower[i][a:a + 1] * lower[i]
        inverse.append(z)
    per = N // BLK
    lane = iota((regions, N), 1)
    for start, block in ((0, lower), (BLK, inverse)):
        for part in range(BLK // per):
            turned = jnp.concatenate(block[part * per:(part + 1) * per], axis=0).T
            for q in range(per):
                row = jnp.where((lane >= q * BLK) & (lane < (q + 1) * BLK), turned, 0.0)
                small_ref[pl.ds(start + part * per + q, regions, stride=2 * BLK), :] = row


def reduce_rows(mat_ref, small_ref, z_ref, m, kb):
    start = pl.multiple_of(m * N + kb, BLK)
    rows = mat_ref[pl.ds(start, BLK), :]
    lane, sub = iota((BLK, N), 1), iota((BLK, N), 0)
    inside = (lane >= kb) & (lane < kb + BLK)
    rows = jnp.where(inside, jnp.where(lane - kb == sub, 1.0, 0.0), rows)
    rh, rl = split(rows)
    sh, sl = split(small_ref[pl.ds(pl.multiple_of(m * 2 * BLK, 2 * BLK), 2 * BLK), :])
    both = mul3(sh, sl, jnp.concatenate([rh] * (N // BLK), axis=0), jnp.concatenate([rl] * (N // BLK), axis=0))
    mat_ref[pl.ds(start, BLK), :] = jnp.where(lane < kb + BLK, both[:BLK], 0.0)
    z_ref[pl.ds(pl.multiple_of(m * BLK, BLK), BLK), :] = both[BLK:]


def mul3(ah, al, bh, bl):
    return jnp.dot(
        jnp.concatenate([ah, al], axis=1), jnp.concatenate([bh, bh], axis=0),
        preferred_element_type=F32,
    ) + jnp.dot(ah, bl, preferred_element_type=F32)


def update(mat_ref, z_ref, m, kb):
    n = N - kb - BLK
    start = pl.multiple_of(m * N + kb + BLK, BLK)
    mat = mat_ref[pl.ds(start, n), :]
    high, low = split(mat)
    zh, zl = split(z_ref[pl.ds(pl.multiple_of(m * BLK, BLK), BLK), :])
    above, below = jnp.zeros((kb, N), BF16), jnp.zeros((n, N), BF16)

    def place(z):
        return jnp.concatenate([p for p in (above, z, below) if p.shape[0]], axis=0)

    change = mul3(high, low, place(zh), place(zl))
    lane = iota((n, N), 1)
    kept = jnp.where((lane >= kb) & (lane < kb + BLK), 0.0, mat)
    mat_ref[pl.ds(start, n), :] = kept - change


def update_kernel(idx_ref, taper_ref, idxv_ref, taperv_ref, pmean_ref, param_ref, *rest):
    chunks = idxv_ref.shape[0] // CHUNK
    parts, rest = rest[:3 * chunks], rest[3 * chunks:]
    (out_ref, wide_ref, mat_ref, small_ref, z_ref, diag_ref, mean_ref, held_ref, made_ref, sems,
     held_sem, made_sems) = rest
    regions, nb = idxv_ref.shape
    ends = 2 * 3 * regions
    copies = []
    for s, src in enumerate(parts):
        copies.append(pltpu.make_async_copy(
            src.at[pl.ds(0, 2 * CHUNK)], wide_ref.at[pl.ds(s * 2 * CHUNK, 2 * CHUNK)], sems.at[2 * s]))
        copies.append(pltpu.make_async_copy(src.at[2 * CHUNK], wide_ref.at[ends + s], sems.at[2 * s + 1]))
    held = pltpu.make_async_copy(param_ref, held_ref, held_sem)
    for c in copies:
        c.start()
    held.start()
    for c in copies:
        c.wait()
    tails = [wide_ref[ends + s].astype(F32) for s in range(3 * chunks)]
    sel_lane = iota((regions, 3 * regions), 1)
    weights = jnp.zeros((regions, 3 * regions), F32)
    for k in range(nb):
        weights = weights + jnp.where(sel_lane == idxv_ref[:, k:k + 1], taperv_ref[:, k:k + 1], 0.0)
    diag_all = jnp.concatenate([t[:CHUNK] for t in tails], axis=0)
    proj_all = jnp.concatenate([t[CHUNK:] for t in tails], axis=0)
    diag_ref[...] = jnp.dot(weights, diag_all, precision=lax.Precision.HIGHEST, preferred_element_type=F32)
    proj = jnp.dot(weights, proj_all, precision=lax.Precision.HIGHEST, preferred_element_type=F32)

    def combine(pair, _):
        packed = []
        for q in range(2):
            r = 2 * pair + q
            acc = None
            for k in range(nb):
                tile = wide_ref[pl.ds(2 * idx_ref[r * nb + k], 2)].reshape(HALF, N)
                term = taper_ref[r * nb + k] * tile.astype(F32)
                acc = term if acc is None else acc + term
            packed.append(acc)
        row = pl.multiple_of(2 * pair * N, N)
        expand(packed, [diag_ref[pl.ds(2 * pair + q, 1), :] for q in range(2)], mat_ref, row, row + N)
        return 0

    lax.fori_loop(0, regions // 2, combine, 0)
    for kb in range(0, N, BLK):
        factor(mat_ref, small_ref, regions, kb)

        def first(t, _, kb=kb):
            for u in range(U1):
                reduce_rows(mat_ref, small_ref, z_ref, t * U1 + u, kb)
            return 0

        def second(t, _, kb=kb):
            for u in range(U2):
                update(mat_ref, z_ref, t * U2 + u, kb)
            return 0

        lax.fori_loop(0, regions // U1, first, 0)
        if kb + BLK < N:
            lax.fori_loop(0, regions // U2, second, 0)

    def weigh(t, mean):
        for u in range(8):
            w = mat_ref[pl.ds(t * 8 + u, regions, stride=N), :]
            mean = mean + jnp.sum(w * proj, axis=1, keepdims=True) * w
        return mean

    mean_ref[...] = lax.fori_loop(0, N // 8, weigh, jnp.zeros((regions, N), F32))

    left_over = pmean_ref[...]
    pieces = []
    for _ in range(3):
        high = left_over.astype(BF16).astype(F32)
        pieces.append(high)
        left_over = left_over - high
    pieces.append(jnp.zeros((N - 3 * regions, left_over.shape[1]), F32))
    columns = jnp.concatenate(pieces, axis=0).T.astype(BF16)
    held.wait()

    def out_copy(m):
        return pltpu.make_async_copy(made_ref.at[m], out_ref.at[m], made_sems.at[m])

    def finish(t, _):
        lane = iota((N, N), 1)
        for u in range(U3):
            m = t * U3 + u
            w = mat_ref[pl.ds(pl.multiple_of(m * N, N), N), :]
            turned = (jnp.sqrt(jnp.float32(N - 1)) * w + mean_ref[pl.ds(m, 1), :]).astype(BF16)
            pick = ((lane == m) | (lane == regions + m) | (lane == 2 * regions + m)).astype(F32).astype(BF16)
            moved = lax.dot_general(
                jnp.concatenate([held_ref[m], columns], axis=1), jnp.concatenate([turned, pick], axis=1),
                (((1,), (1,)), ((), ())), preferred_element_type=F32,
            )
            made_ref[m] = moved.astype(BF16)
        for u in range(U3):
            out_copy(t * U3 + u).start()
        return 0

    lax.fori_loop(0, regions // U3, finish, 0)
    for m in range(regions):
        out_copy(m).wait()


def solve_update(idx, taper, parts, param_mean, param_anomaly):
    regions, nb = idx.shape
    hbm = pl.BlockSpec(memory_space=pl.ANY)
    smem = pl.BlockSpec(memory_space=pltpu.SMEM)
    vmem = pl.BlockSpec(memory_space=pltpu.VMEM)
    return pl.pallas_call(
        update_kernel,
        out_shape=jax.ShapeDtypeStruct(param_anomaly.shape, BF16),
        in_specs=[smem, smem, vmem, vmem, vmem, hbm] + [hbm] * len(parts),
        out_specs=hbm,
        scratch_shapes=[
            pltpu.VMEM((6 * regions + len(parts), HALF // 2, N), BF16),
            pltpu.VMEM((regions * N, N), F32),
            pltpu.VMEM((regions * 2 * BLK, N), F32),
            pltpu.VMEM((regions * BLK, N), F32),
            pltpu.VMEM((regions, N), F32),
            pltpu.VMEM((regions, N), F32),
            pltpu.VMEM(param_anomaly.shape, BF16),
            pltpu.VMEM(param_anomaly.shape, BF16),
            pltpu.SemaphoreType.DMA((2 * len(parts),)),
            pltpu.SemaphoreType.DMA,
            pltpu.SemaphoreType.DMA((regions,)),
        ],
        compiler_params=pltpu.CompilerParams(vmem_limit_bytes=56 << 20),
        name="solve_update",
    )(idx.reshape(-1), taper.reshape(-1), idx, taper, param_mean, param_anomaly, *parts)


def body(obs_anomaly, innovation, obs_count, neighbour, taper, param_anomaly, param_mean):
    regions, slots = obs_anomaly.shape[:2]
    size, half = lax.axis_size("region"), lax.axis_size("obs")
    total = regions * size
    here, part = lax.axis_index("region"), lax.axis_index("obs")
    devices = [(r, o) for r in range(size) for o in range(half)]

    def swap(x, other):
        line = [(r * half + o, (lambda a: (a[0] % size) * half + a[1])(other(r, o))) for r, o in devices]
        return lax.ppermute(x, ("region", "obs"), line)

    own, near, far = [], [], []
    live = obs_count - part * slots
    for first in range(0, regions, CHUNK):
        packed = grams(live, obs_anomaly, innovation, first)
        partner = swap(packed, lambda r, o: (r, 1 - o))
        both = (packed.astype(F32) + partner.astype(F32)).astype(BF16)
        own.append(both)
        far.append(swap(both, lambda r, o: (r + 1 if r % 2 else r - 1, 1 - o)))
        near.append(swap(both, lambda r, o: (r ^ 1, o)))
    place = (neighbour - here * regions + regions) % total
    even = here % 2 == 0
    before, after = jnp.where(even, 2, 1), jnp.where(even, 1, 2)
    slot = jnp.where(place < regions, before, jnp.where(place < 2 * regions, 0, after))
    idx = (slot * regions + place % regions).astype(jnp.int32)
    return solve_update(idx, taper, own + near + far, param_mean, param_anomaly)


def solution(mesh):
    specs = (
        P("region", "obs", None), P("region", "obs"), P("region"), P("region", None),
        P("region", None), P("region", "obs", None), P("region", "obs"),
    )
    return jax.shard_map(body, mesh=mesh, in_specs=specs, out_specs=P("region", "obs", None), check_vma=False)
```

```python
import functools

import jax
import jax.numpy as jnp
from jax import lax
from jax.experimental import pallas as pl
from jax.experimental.pallas import tpu as pltpu
from jax.sharding import PartitionSpec as P

N = 128
HALF = 64
CHUNK = 16
BLK = 16
U1, U2, U3 = 32, 32, 8
F32 = jnp.float32
BF16 = jnp.bfloat16


def iota(shape, dim):
    return lax.broadcasted_iota(jnp.int32, shape, dim)


def pack(gram):
    top, bottom = gram[:HALF], pltpu.roll(gram[HALF:], HALF, 1)
    return jnp.where(iota((HALF, N), 1) >= iota((HALF, N), 0), top, bottom)


def gram_kernel(step, first, count_ref, y_ref, d_ref, out_ref, diag_ref, proj_ref):
    slots = y_ref.shape[1]
    total = diag_ref.shape[0]
    base = pl.program_id(0) * step
    rows = lax.broadcasted_iota(jnp.int16, (slots, N), 0)
    on_ridge = iota((HALF, N), 0) + HALF == iota((HALF, N), 1)
    start = pl.multiple_of((base // 16) * 16, 16)
    drows = iota((16, N), 0)
    d = d_ref[pl.ds(pl.multiple_of(first + start, 16), 16), :]
    for s in range(step):
        r = base + s
        live = jnp.clip(count_ref[first + r] - lax.axis_index("obs") * slots, 0, slots).astype(jnp.int16)
        y = jnp.where(rows < live, y_ref[s], jnp.zeros((), BF16))
        full = jnp.dot(jnp.concatenate([y.T, d], axis=0), y, preferred_element_type=F32)
        packed = pack(full[:N]).astype(BF16)
        out_ref[2 * r] = packed[:HALF // 2]
        out_ref[2 * r + 1] = packed[HALF // 2:]
        diag_ref[pl.ds(r, 1), :] = jnp.sum(jnp.where(on_ridge, full[HALF:N], 0.0), axis=0, keepdims=True)
        proj_ref[pl.ds(r, 1), :] = jnp.sum(jnp.where(drows == r - start, full[N:], 0.0), axis=0, keepdims=True)

    @pl.when(pl.program_id(0) == pl.num_programs(0) - 1)
    def _():
        out_ref[2 * total] = jnp.concatenate([diag_ref[...], proj_ref[...]], axis=0).astype(BF16)


def grams(obs_count, obs_anomaly, innovation, first, step=8):
    regions, slots, _ = obs_anomaly.shape
    return pl.pallas_call(
        functools.partial(gram_kernel, step, first),
        out_shape=jax.ShapeDtypeStruct((2 * CHUNK + 1, HALF // 2, N), BF16),
        grid_spec=pltpu.PrefetchScalarGridSpec(
            num_scalar_prefetch=1,
            grid=(CHUNK // step,),
            in_specs=[
                pl.BlockSpec((step, slots, N), lambda i, c: (i + first // step, 0, 0)),
                pl.BlockSpec((regions, slots), lambda i, c: (0, 0)),
            ],
            out_specs=pl.BlockSpec((2 * CHUNK + 1, HALF // 2, N), lambda i, c: (0, 0, 0)),
            scratch_shapes=[pltpu.VMEM((CHUNK, N), F32), pltpu.VMEM((CHUNK, N), F32)],
        ),
        compiler_params=pltpu.CompilerParams(vmem_limit_bytes=48 << 20),
        name="grams",
    )(obs_count, obs_anomaly, innovation)


def split(x):
    high = x.astype(BF16)
    return high, (x - high.astype(F32)).astype(BF16)


def expand(pair_packed, diags, mat_ref, row_a, row_b):
    la, lb = pair_packed
    i, j = iota((HALF, N), 0), iota((HALF, N), 1)
    turned = jnp.concatenate([la, lb], axis=0).T
    top, bottom = turned[:HALF], turned[HALF:]
    top_r, bottom_r = pltpu.roll(top, HALF, 1), pltpu.roll(bottom, HALF, 1)
    ridge = jnp.where(i == j, N - 1.0, 0.0)
    for row, lp, tt, tl, tr, dg in (
        (row_a, la, top, bottom, top_r, diags[0]), (row_b, lb, top_r, bottom_r, top, diags[1]),
    ):
        mat_ref[pl.ds(row, HALF), :] = jnp.where(i <= j, lp, tt) + ridge
        corner = jnp.where(i + HALF > j, pltpu.roll(lp, HALF, 1), tr)
        corner = jnp.where(i + HALF == j, dg + (N - 1.0), corner)
        mat_ref[pl.ds(row + HALF, HALF), :] = jnp.where(j < HALF, tl, corner)


def factor(mat_ref, small_ref, regions, kb):
    sub = iota((BLK, regions), 0)
    x = []
    for i in range(BLK):
        row = mat_ref[pl.ds(kb + i, regions, stride=N), :]
        x.append(row.T[kb:kb + BLK])
    lower = []
    for i in range(BLK):
        scale = lax.rsqrt(x[i][i:i + 1])
        r = jnp.where(sub == i, 1.0, x[i]) * scale
        for j in range(i + 1, BLK):
            x[j] = jnp.where(sub == i, 0.0, x[j]) - (x[i][j:j + 1] * scale) * r
        lower.append(jnp.where(sub <= i, r, 0.0))
    inverse = []
    for a in range(BLK):
        z = lower[a][a:a + 1] * lower[a]
        for i in range(a + 1, BLK):
            z = z + lower[i][a:a + 1] * lower[i]
        inverse.append(z)
    per = N // BLK
    lane = iota((regions, N), 1)
    for start, block in ((0, lower), (BLK, inverse)):
        for part in range(BLK // per):
            turned = jnp.concatenate(block[part * per:(part + 1) * per], axis=0).T
            for q in range(per):
                row = jnp.where((lane >= q * BLK) & (lane < (q + 1) * BLK), turned, 0.0)
                small_ref[pl.ds(start + part * per + q, regions, stride=2 * BLK), :] = row


def reduce_rows(mat_ref, small_ref, z_ref, m, kb):
    start = pl.multiple_of(m * N + kb, BLK)
    rows = mat_ref[pl.ds(start, BLK), :]
    lane, sub = iota((BLK, N), 1), iota((BLK, N), 0)
    inside = (lane >= kb) & (lane < kb + BLK)
    rows = jnp.where(inside, jnp.where(lane - kb == sub, 1.0, 0.0), rows)
    rh, rl = split(rows)
    sh, sl = split(small_ref[pl.ds(pl.multiple_of(m * 2 * BLK, 2 * BLK), 2 * BLK), :])
    both = mul_m(sh, sl, jnp.concatenate([rh] * (N // BLK), axis=0), jnp.concatenate([rl] * (N // BLK), axis=0))
    mat_ref[pl.ds(start, BLK), :] = jnp.where(lane < kb + BLK, both[:BLK], 0.0)
    z_ref[pl.ds(pl.multiple_of(m * BLK, BLK), BLK), :] = both[BLK:]


def mul_k(ah, al, bh, bl):
    right = jnp.concatenate([
        jnp.concatenate([bh, bl], axis=1), jnp.concatenate([bh, jnp.zeros_like(bl)], axis=1)], axis=0)
    both = jnp.dot(jnp.concatenate([ah, al], axis=1), right, preferred_element_type=F32)
    return both[:, :N] + both[:, N:]


def mul_m(ah, al, bh, bl):
    n = ah.shape[0]
    both = jnp.dot(jnp.concatenate([ah, al], axis=0), jnp.concatenate([bh, bl], axis=1), preferred_element_type=F32)
    return (both[:n, :N] + both[:n, N:]) + both[n:, :N]


def update(mat_ref, z_ref, m, kb):
    n = N - kb - BLK
    start = pl.multiple_of(m * N + kb + BLK, BLK)
    mat = mat_ref[pl.ds(start, n), :]
    high, low = split(mat)
    zh, zl = split(z_ref[pl.ds(pl.multiple_of(m * BLK, BLK), BLK), :])
    above, below = jnp.zeros((kb, N), BF16), jnp.zeros((n, N), BF16)

    def place(z):
        return jnp.concatenate([p for p in (above, z, below) if p.shape[0]], axis=0)

    change = mul_k(high, low, place(zh), place(zl))
    lane = iota((n, N), 1)
    kept = jnp.where((lane >= kb) & (lane < kb + BLK), 0.0, mat)
    mat_ref[pl.ds(start, n), :] = kept - change


def update_kernel(idx_ref, taper_ref, idxv_ref, taperv_ref, pmean_ref, param_ref, *rest):
    chunks = idxv_ref.shape[0] // CHUNK
    parts, rest = rest[:3 * chunks], rest[3 * chunks:]
    (out_ref, wide_ref, mat_ref, small_ref, z_ref, diag_ref, mean_ref, held_ref, made_ref, sems,
     held_sem, made_sems) = rest
    regions, nb = idxv_ref.shape
    ends = 2 * 3 * regions
    copies = []
    for s, src in enumerate(parts):
        copies.append(pltpu.make_async_copy(
            src.at[pl.ds(0, 2 * CHUNK)], wide_ref.at[pl.ds(s * 2 * CHUNK, 2 * CHUNK)], sems.at[2 * s]))
        copies.append(pltpu.make_async_copy(src.at[2 * CHUNK], wide_ref.at[ends + s], sems.at[2 * s + 1]))
    held = pltpu.make_async_copy(param_ref, held_ref, held_sem)
    for c in copies:
        c.start()
    held.start()
    for c in copies:
        c.wait()
    tails = [wide_ref[ends + s].astype(F32) for s in range(3 * chunks)]
    sel_lane = iota((regions, 3 * regions), 1)
    weights = jnp.zeros((regions, 3 * regions), F32)
    for k in range(nb):
        weights = weights + jnp.where(sel_lane == idxv_ref[:, k:k + 1], taperv_ref[:, k:k + 1], 0.0)
    diag_all = jnp.concatenate([t[:CHUNK] for t in tails], axis=0)
    proj_all = jnp.concatenate([t[CHUNK:] for t in tails], axis=0)
    diag_ref[...] = jnp.dot(weights, diag_all, precision=lax.Precision.HIGHEST, preferred_element_type=F32)
    proj = jnp.dot(weights, proj_all, precision=lax.Precision.HIGHEST, preferred_element_type=F32)

    def combine(pair, _):
        packed = []
        for q in range(2):
            r = 2 * pair + q
            acc = None
            for k in range(nb):
                tile = wide_ref[pl.ds(2 * idx_ref[r, k], 2)].reshape(HALF, N)
                term = taper_ref[r, k] * tile.astype(F32)
                acc = term if acc is None else acc + term
            packed.append(acc)
        row = pl.multiple_of(2 * pair * N, N)
        expand(packed, [diag_ref[pl.ds(2 * pair + q, 1), :] for q in range(2)], mat_ref, row, row + N)
        return 0

    lax.fori_loop(0, regions // 2, combine, 0, unroll=8)
    for kb in range(0, N, BLK):
        factor(mat_ref, small_ref, regions, kb)

        def first(t, _, kb=kb):
            for u in range(U1):
                reduce_rows(mat_ref, small_ref, z_ref, t * U1 + u, kb)
            return 0

        def second(t, _, kb=kb):
            for u in range(U2):
                update(mat_ref, z_ref, t * U2 + u, kb)
            return 0

        lax.fori_loop(0, regions // U1, first, 0)
        if kb + BLK < N:
            lax.fori_loop(0, regions // U2, second, 0)

    def weigh(t, mean):
        for u in range(32):
            w = mat_ref[pl.ds(t * 32 + u, regions, stride=N), :]
            mean = mean + jnp.sum(w * proj, axis=1, keepdims=True) * w
        return mean

    mean_ref[...] = lax.fori_loop(0, N // 32, weigh, jnp.zeros((regions, N), F32))

    left_over = pmean_ref[...]
    pieces = []
    for _ in range(3):
        high = left_over.astype(BF16).astype(F32)
        pieces.append(high)
        left_over = left_over - high
    pieces.append(jnp.zeros((N - 3 * regions, left_over.shape[1]), F32))
    columns = jnp.concatenate(pieces, axis=0).T.astype(BF16)
    held.wait()

    def out_copy(m):
        return pltpu.make_async_copy(made_ref.at[m], out_ref.at[m], made_sems.at[m])

    def finish(t, _):
        lane = iota((N, N), 1)
        for u in range(U3):
            m = t * U3 + u
            w = mat_ref[pl.ds(pl.multiple_of(m * N, N), N), :]
            turned = (jnp.sqrt(jnp.float32(N - 1)) * w + mean_ref[pl.ds(m, 1), :]).astype(BF16)
            pick = ((lane == m) | (lane == regions + m) | (lane == 2 * regions + m)).astype(F32).astype(BF16)
            moved = lax.dot_general(
                jnp.concatenate([held_ref[m], columns], axis=1), jnp.concatenate([turned, pick], axis=1),
                (((1,), (1,)), ((), ())), preferred_element_type=F32,
            )
            made_ref[m] = moved.astype(BF16)
        for u in range(U3):
            out_copy(t * U3 + u).start()
        return 0

    lax.fori_loop(0, regions // U3, finish, 0)
    for m in range(regions):
        out_copy(m).wait()


def solve_update(idx, taper, parts, param_mean, param_anomaly):
    regions, nb = idx.shape
    hbm = pl.BlockSpec(memory_space=pl.ANY)
    smem = pl.BlockSpec(memory_space=pltpu.SMEM)
    vmem = pl.BlockSpec(memory_space=pltpu.VMEM)
    return pl.pallas_call(
        update_kernel,
        out_shape=jax.ShapeDtypeStruct(param_anomaly.shape, BF16),
        in_specs=[smem, smem, vmem, vmem, vmem, hbm] + [hbm] * len(parts),
        out_specs=hbm,
        scratch_shapes=[
            pltpu.VMEM((6 * regions + len(parts), HALF // 2, N), BF16),
            pltpu.VMEM((regions * N, N), F32),
            pltpu.VMEM((regions * 2 * BLK, N), F32),
            pltpu.VMEM((regions * BLK, N), F32),
            pltpu.VMEM((regions, N), F32),
            pltpu.VMEM((regions, N), F32),
            pltpu.VMEM(param_anomaly.shape, BF16),
            pltpu.VMEM(param_anomaly.shape, BF16),
            pltpu.SemaphoreType.DMA((2 * len(parts),)),
            pltpu.SemaphoreType.DMA,
            pltpu.SemaphoreType.DMA((regions,)),
        ],
        compiler_params=pltpu.CompilerParams(vmem_limit_bytes=56 << 20),
        name="solve_update",
    )(idx, taper, idx, taper, param_mean, param_anomaly, *parts)


def body(obs_anomaly, innovation, obs_count, neighbour, taper, param_anomaly, param_mean):
    regions = obs_anomaly.shape[0]
    size, half = lax.axis_size("region"), lax.axis_size("obs")
    total = regions * size
    here = lax.axis_index("region")
    devices = [(r, o) for r in range(size) for o in range(half)]

    def swap(x, other):
        line = [(r * half + o, (lambda a: (a[0] % size) * half + a[1])(other(r, o))) for r, o in devices]
        return lax.ppermute(x, ("region", "obs"), line)

    own, near, far = [], [], []
    for first in range(0, regions, CHUNK):
        packed = grams(obs_count, obs_anomaly, innovation, first)
        partner = swap(packed, lambda r, o: (r, 1 - o))
        both = (packed.astype(F32) + partner.astype(F32)).astype(BF16)
        own.append(both)
        far.append(swap(both, lambda r, o: (r + 1 if r % 2 else r - 1, 1 - o)))
        near.append(swap(both, lambda r, o: (r ^ 1, o)))
    place = (neighbour - here * regions + regions) % total
    even = here % 2 == 0
    before, after = jnp.where(even, 2, 1), jnp.where(even, 1, 2)
    slot = jnp.where(place < regions, before, jnp.where(place < 2 * regions, 0, after))
    idx = (slot * regions + place % regions).astype(jnp.int32)
    return solve_update(idx, taper, own + near + far, param_mean, param_anomaly)


def solution(mesh):
    specs = (
        P("region", "obs", None), P("region", "obs"), P("region"), P("region", None),
        P("region", None), P("region", "obs", None), P("region", "obs"),
    )
    return jax.shard_map(body, mesh=mesh, in_specs=specs, out_specs=P("region", "obs", None), check_vma=False)
```

```python
import functools

import jax
import jax.numpy as jnp
from jax import lax
from jax.experimental import pallas as pl
from jax.experimental.pallas import tpu as pltpu
from jax.sharding import PartitionSpec as P

N = 128
HALF = 64
CHUNK = 16
BLK = 16
U1, U2, U3 = 32, 32, 8
F32 = jnp.float32
BF16 = jnp.bfloat16


def iota(shape, dim):
    return lax.broadcasted_iota(jnp.int32, shape, dim)


def pack(gram):
    top, bottom = gram[:HALF], pltpu.roll(gram[HALF:], HALF, 1)
    return jnp.where(iota((HALF, N), 1) >= iota((HALF, N), 0), top, bottom)


def gram_kernel(step, first, count_hbm, y_hbm, d_hbm, out_ref, count_ref, y_ref, d_ref, diag_ref, proj_ref,
                y_sems, sems):
    total, slots = y_ref.shape[:2]
    small = [
        pltpu.make_async_copy(count_hbm, count_ref, sems.at[0]),
        pltpu.make_async_copy(d_hbm.at[pl.ds(first, total)], d_ref, sems.at[1]),
    ]

    def fetch(r):
        return pltpu.make_async_copy(y_hbm.at[first + r], y_ref.at[r], y_sems.at[r])

    small[0].start()
    fetch(0).start()
    small[1].start()
    for r in range(1, total):
        fetch(r).start()
    small[0].wait()
    small[1].wait()
    base = lax.axis_index("obs") * slots
    rows = lax.broadcasted_iota(jnp.int16, (slots, N), 0)
    on_ridge = iota((HALF, N), 0) + HALF == iota((HALF, N), 1)
    drows = iota((total, N), 0)

    def some(t, _):
        for s in range(step):
            fetch(t * step + s).wait()
        for s in range(step):
            r = t * step + s
            live = jnp.clip(count_ref[first + r] - base, 0, slots).astype(jnp.int16)
            y = jnp.where(rows < live, y_ref[r], jnp.zeros((), BF16))
            full = jnp.dot(jnp.concatenate([y.T, d_ref[...]], axis=0), y, preferred_element_type=F32)
            packed = pack(full[:N]).astype(BF16)
            out_ref[2 * r] = packed[:HALF // 2]
            out_ref[2 * r + 1] = packed[HALF // 2:]
            diag_ref[pl.ds(r, 1), :] = jnp.sum(jnp.where(on_ridge, full[HALF:N], 0.0), axis=0, keepdims=True)
            proj_ref[pl.ds(r, 1), :] = jnp.sum(jnp.where(drows == r, full[N:], 0.0), axis=0, keepdims=True)
        return 0

    lax.fori_loop(0, total // step, some, 0)
    out_ref[2 * total] = jnp.concatenate([diag_ref[...], proj_ref[...]], axis=0).astype(BF16)


def grams(obs_count, obs_anomaly, innovation, first, step=8):
    regions, slots, _ = obs_anomaly.shape
    hbm = pl.BlockSpec(memory_space=pltpu.HBM)
    return pl.pallas_call(
        functools.partial(gram_kernel, step, first),
        out_shape=jax.ShapeDtypeStruct((2 * CHUNK + 1, HALF // 2, N), BF16),
        in_specs=[hbm, hbm, hbm],
        out_specs=pl.BlockSpec(memory_space=pltpu.VMEM),
        scratch_shapes=[
            pltpu.SMEM((regions,), jnp.int32),
            pltpu.VMEM((CHUNK, slots, N), BF16),
            pltpu.VMEM((CHUNK, slots), BF16),
            pltpu.VMEM((CHUNK, N), F32),
            pltpu.VMEM((CHUNK, N), F32),
            pltpu.SemaphoreType.DMA((CHUNK,)),
            pltpu.SemaphoreType.DMA((2,)),
        ],
        compiler_params=pltpu.CompilerParams(vmem_limit_bytes=63 << 20),
        name="grams",
    )(obs_count, obs_anomaly, innovation)


def split(x):
    high = x.astype(BF16)
    return high, (x - high.astype(F32)).astype(BF16)


def expand(pair_packed, diags, mat_ref, row_a, row_b):
    la, lb = pair_packed
    i, j = iota((HALF, N), 0), iota((HALF, N), 1)
    turned = jnp.concatenate([la, lb], axis=0).T
    top, bottom = turned[:HALF], turned[HALF:]
    top_r, bottom_r = pltpu.roll(top, HALF, 1), pltpu.roll(bottom, HALF, 1)
    ridge = jnp.where(i == j, N - 1.0, 0.0)
    for row, lp, tt, tl, tr, dg in (
        (row_a, la, top, bottom, top_r, diags[0]), (row_b, lb, top_r, bottom_r, top, diags[1]),
    ):
        mat_ref[pl.ds(row, HALF), :] = jnp.where(i <= j, lp, tt) + ridge
        corner = jnp.where(i + HALF > j, pltpu.roll(lp, HALF, 1), tr)
        corner = jnp.where(i + HALF == j, dg + (N - 1.0), corner)
        mat_ref[pl.ds(row + HALF, HALF), :] = jnp.where(j < HALF, tl, corner)


def factor(mat_ref, small_ref, regions, kb):
    sub = iota((BLK, regions), 0)
    x = []
    for i in range(BLK):
        row = mat_ref[pl.ds(kb + i, regions, stride=N), :]
        x.append(row.T[kb:kb + BLK])
    lower = []
    for i in range(BLK):
        scale = lax.rsqrt(x[i][i:i + 1])
        r = jnp.where(sub == i, 1.0, x[i]) * scale
        for j in range(i + 1, BLK):
            x[j] = jnp.where(sub == i, 0.0, x[j]) - (x[i][j:j + 1] * scale) * r
        lower.append(jnp.where(sub <= i, r, 0.0))
    inverse = []
    for a in range(BLK):
        z = lower[a][a:a + 1] * lower[a]
        for i in range(a + 1, BLK):
            z = z + lower[i][a:a + 1] * lower[i]
        inverse.append(z)
    per = N // BLK
    lane = iota((regions, N), 1)
    for start, block in ((0, lower), (BLK, inverse)):
        for part in range(BLK // per):
            turned = jnp.concatenate(block[part * per:(part + 1) * per], axis=0).T
            for q in range(per):
                row = jnp.where((lane >= q * BLK) & (lane < (q + 1) * BLK), turned, 0.0)
                small_ref[pl.ds(start + part * per + q, regions, stride=2 * BLK), :] = row


def reduce_rows(mat_ref, small_ref, z_ref, m, kb):
    start = pl.multiple_of(m * N + kb, BLK)
    rows = mat_ref[pl.ds(start, BLK), :]
    lane, sub = iota((BLK, N), 1), iota((BLK, N), 0)
    inside = (lane >= kb) & (lane < kb + BLK)
    rows = jnp.where(inside, jnp.where(lane - kb == sub, 1.0, 0.0), rows)
    rh, rl = split(rows)
    sh, sl = split(small_ref[pl.ds(pl.multiple_of(m * 2 * BLK, 2 * BLK), 2 * BLK), :])
    both = mul_m(sh, sl, jnp.concatenate([rh] * (N // BLK), axis=0), jnp.concatenate([rl] * (N // BLK), axis=0))
    mat_ref[pl.ds(start, BLK), :] = jnp.where(lane < kb + BLK, both[:BLK], 0.0)
    z_ref[pl.ds(pl.multiple_of(m * BLK, BLK), BLK), :] = both[BLK:]


def mul_k(ah, al, bh, bl):
    right = jnp.concatenate([
        jnp.concatenate([bh, bl], axis=1), jnp.concatenate([bh, jnp.zeros_like(bl)], axis=1)], axis=0)
    both = jnp.dot(jnp.concatenate([ah, al], axis=1), right, preferred_element_type=F32)
    return both[:, :N] + both[:, N:]


def mul_m(ah, al, bh, bl):
    n = ah.shape[0]
    both = jnp.dot(jnp.concatenate([ah, al], axis=0), jnp.concatenate([bh, bl], axis=1), preferred_element_type=F32)
    return (both[:n, :N] + both[:n, N:]) + both[n:, :N]


def update(mat_ref, z_ref, m, kb):
    n = N - kb - BLK
    start = pl.multiple_of(m * N + kb + BLK, BLK)
    mat = mat_ref[pl.ds(start, n), :]
    high, low = split(mat)
    zh, zl = split(z_ref[pl.ds(pl.multiple_of(m * BLK, BLK), BLK), :])
    above, below = jnp.zeros((kb, N), BF16), jnp.zeros((n, N), BF16)

    def place(z):
        return jnp.concatenate([p for p in (above, z, below) if p.shape[0]], axis=0)

    change = mul_k(high, low, place(zh), place(zl))
    lane = iota((n, N), 1)
    kept = jnp.where((lane >= kb) & (lane < kb + BLK), 0.0, mat)
    mat_ref[pl.ds(start, n), :] = kept - change


def update_kernel(idx_ref, taper_ref, idxv_ref, taperv_ref, pmean_ref, param_ref, *rest):
    chunks = idxv_ref.shape[0] // CHUNK
    parts, rest = rest[:3 * chunks], rest[3 * chunks:]
    (out_ref, wide_ref, mat_ref, small_ref, z_ref, diag_ref, mean_ref, held_ref, made_ref,
     held_sem, made_sems) = rest
    regions, nb = idxv_ref.shape
    held = pltpu.make_async_copy(param_ref, held_ref, held_sem)
    held.start()
    for s, src in enumerate(parts):
        wide_ref[pl.ds(s * 2 * CHUNK, 2 * CHUNK)] = src[pl.ds(0, 2 * CHUNK)]
    tails = [src[2 * CHUNK].astype(F32) for src in parts]
    sel_lane = iota((regions, 3 * regions), 1)
    weights = jnp.zeros((regions, 3 * regions), F32)
    for k in range(nb):
        weights = weights + jnp.where(sel_lane == idxv_ref[:, k:k + 1], taperv_ref[:, k:k + 1], 0.0)
    diag_all = jnp.concatenate([t[:CHUNK] for t in tails], axis=0)
    proj_all = jnp.concatenate([t[CHUNK:] for t in tails], axis=0)
    diag_ref[...] = jnp.dot(weights, diag_all, precision=lax.Precision.HIGHEST, preferred_element_type=F32)
    proj = jnp.dot(weights, proj_all, precision=lax.Precision.HIGHEST, preferred_element_type=F32)

    def combine(pair, _):
        packed = []
        for q in range(2):
            r = 2 * pair + q
            acc = None
            for k in range(nb):
                tile = wide_ref[pl.ds(2 * idx_ref[r, k], 2)].reshape(HALF, N)
                term = taper_ref[r, k] * tile.astype(F32)
                acc = term if acc is None else acc + term
            packed.append(acc)
        row = pl.multiple_of(2 * pair * N, N)
        expand(packed, [diag_ref[pl.ds(2 * pair + q, 1), :] for q in range(2)], mat_ref, row, row + N)
        return 0

    lax.fori_loop(0, regions // 2, combine, 0, unroll=8)
    for kb in range(0, N, BLK):
        factor(mat_ref, small_ref, regions, kb)

        def first(t, _, kb=kb):
            for u in range(U1):
                reduce_rows(mat_ref, small_ref, z_ref, t * U1 + u, kb)
            return 0

        def second(t, _, kb=kb):
            for u in range(U2):
                update(mat_ref, z_ref, t * U2 + u, kb)
            return 0

        lax.fori_loop(0, regions // U1, first, 0)
        if kb + BLK < N:
            lax.fori_loop(0, regions // U2, second, 0)

    def weigh(t, mean):
        for u in range(32):
            w = mat_ref[pl.ds(t * 32 + u, regions, stride=N), :]
            mean = mean + jnp.sum(w * proj, axis=1, keepdims=True) * w
        return mean

    mean_ref[...] = lax.fori_loop(0, N // 32, weigh, jnp.zeros((regions, N), F32))

    left_over = pmean_ref[...]
    pieces = []
    for _ in range(3):
        high = left_over.astype(BF16).astype(F32)
        pieces.append(high)
        left_over = left_over - high
    pieces.append(jnp.zeros((N - 3 * regions, left_over.shape[1]), F32))
    columns = jnp.concatenate(pieces, axis=0).T.astype(BF16)
    held.wait()

    def out_copy(m):
        return pltpu.make_async_copy(made_ref.at[m], out_ref.at[m], made_sems.at[m])

    def finish(t, _):
        lane = iota((N, N), 1)
        for u in range(U3):
            m = t * U3 + u
            w = mat_ref[pl.ds(pl.multiple_of(m * N, N), N), :]
            turned = (jnp.sqrt(jnp.float32(N - 1)) * w + mean_ref[pl.ds(m, 1), :]).astype(BF16)
            pick = ((lane == m) | (lane == regions + m) | (lane == 2 * regions + m)).astype(F32).astype(BF16)
            moved = lax.dot_general(
                jnp.concatenate([held_ref[m], columns], axis=1), jnp.concatenate([turned, pick], axis=1),
                (((1,), (1,)), ((), ())), preferred_element_type=F32,
            )
            made_ref[m] = moved.astype(BF16)
        for u in range(U3):
            out_copy(t * U3 + u).start()
        return 0

    lax.fori_loop(0, regions // U3, finish, 0)
    for m in range(regions):
        out_copy(m).wait()


def solve_update(idx, taper, parts, param_mean, param_anomaly):
    regions, nb = idx.shape
    hbm = pl.BlockSpec(memory_space=pl.ANY)
    smem = pl.BlockSpec(memory_space=pltpu.SMEM)
    vmem = pl.BlockSpec(memory_space=pltpu.VMEM)
    return pl.pallas_call(
        update_kernel,
        out_shape=jax.ShapeDtypeStruct(param_anomaly.shape, BF16),
        in_specs=[smem, smem, vmem, vmem, vmem, hbm] + [vmem] * len(parts),
        out_specs=hbm,
        scratch_shapes=[
            pltpu.VMEM((6 * regions, HALF // 2, N), BF16),
            pltpu.VMEM((regions * N, N), F32),
            pltpu.VMEM((regions * 2 * BLK, N), F32),
            pltpu.VMEM((regions * BLK, N), F32),
            pltpu.VMEM((regions, N), F32),
            pltpu.VMEM((regions, N), F32),
            pltpu.VMEM(param_anomaly.shape, BF16),
            pltpu.VMEM(param_anomaly.shape, BF16),
            pltpu.SemaphoreType.DMA,
            pltpu.SemaphoreType.DMA((regions,)),
        ],
        compiler_params=pltpu.CompilerParams(vmem_limit_bytes=48 << 20),
        name="solve_update",
    )(idx, taper, idx, taper, param_mean, param_anomaly, *parts)


def body(obs_anomaly, innovation, obs_count, neighbour, taper, param_anomaly, param_mean):
    regions = obs_anomaly.shape[0]
    size, half = lax.axis_size("region"), lax.axis_size("obs")
    total = regions * size
    here = lax.axis_index("region")
    devices = [(r, o) for r in range(size) for o in range(half)]

    def swap(x, other):
        line = [(r * half + o, (lambda a: (a[0] % size) * half + a[1])(other(r, o))) for r, o in devices]
        return lax.ppermute(x, ("region", "obs"), line)

    own, near, far = [], [], []
    for first in range(0, regions, CHUNK):
        packed = grams(obs_count, obs_anomaly, innovation, first)
        partner = swap(packed, lambda r, o: (r, 1 - o))
        both = (packed.astype(F32) + partner.astype(F32)).astype(BF16)
        own.append(both)
        far.append(swap(both, lambda r, o: (r + 1 if r % 2 else r - 1, 1 - o)))
        near.append(swap(both, lambda r, o: (r ^ 1, o)))
    place = (neighbour - here * regions + regions) % total
    even = here % 2 == 0
    before, after = jnp.where(even, 2, 1), jnp.where(even, 1, 2)
    slot = jnp.where(place < regions, before, jnp.where(place < 2 * regions, 0, after))
    idx = (slot * regions + place % regions).astype(jnp.int32)
    return solve_update(idx, taper, own + near + far, param_mean, param_anomaly)


def solution(mesh):
    specs = (
        P("region", "obs", None), P("region", "obs"), P("region"), P("region", None),
        P("region", None), P("region", "obs", None), P("region", "obs"),
    )
    return jax.shard_map(body, mesh=mesh, in_specs=specs, out_specs=P("region", "obs", None), check_vma=False)
```

```python
import functools

import jax
import jax.numpy as jnp
from jax import lax
from jax.experimental import pallas as pl
from jax.experimental.pallas import tpu as pltpu
from jax.sharding import PartitionSpec as P

N = 128
HALF = 64
CHUNK = 16
BLK = 16
U3 = 8
F32 = jnp.float32
BF16 = jnp.bfloat16


def iota(shape, dim):
    return lax.broadcasted_iota(jnp.int32, shape, dim)


def pack(gram):
    top, bottom = gram[:HALF], pltpu.roll(gram[HALF:], HALF, 1)
    return jnp.where(iota((HALF, N), 1) >= iota((HALF, N), 0), top, bottom)


def gram_kernel(step, first, count_hbm, y_hbm, d_hbm, out_ref, count_ref, y_ref, d_ref, diag_ref, proj_ref,
                y_sems, sems):
    total, slots = y_ref.shape[:2]
    small = [
        pltpu.make_async_copy(count_hbm, count_ref, sems.at[0]),
        pltpu.make_async_copy(d_hbm.at[pl.ds(first, total)], d_ref, sems.at[1]),
    ]

    def fetch(r):
        return pltpu.make_async_copy(y_hbm.at[first + r], y_ref.at[r], y_sems.at[r])

    small[0].start()
    fetch(0).start()
    small[1].start()
    for r in range(1, total):
        fetch(r).start()
    small[0].wait()
    small[1].wait()
    base = lax.axis_index("obs") * slots
    rows = lax.broadcasted_iota(jnp.int16, (slots, N), 0)
    on_ridge = iota((HALF, N), 0) + HALF == iota((HALF, N), 1)
    drows = iota((total, N), 0)

    def some(t, _):
        for s in range(step):
            fetch(t * step + s).wait()
        for s in range(step):
            r = t * step + s
            live = jnp.clip(count_ref[first + r] - base, 0, slots).astype(jnp.int16)
            y = jnp.where(rows < live, y_ref[r], jnp.zeros((), BF16))
            full = jnp.dot(jnp.concatenate([y.T, d_ref[...]], axis=0), y, preferred_element_type=F32)
            packed = pack(full[:N]).astype(BF16)
            out_ref[2 * r] = packed[:HALF // 2]
            out_ref[2 * r + 1] = packed[HALF // 2:]
            diag_ref[pl.ds(r, 1), :] = jnp.sum(jnp.where(on_ridge, full[HALF:N], 0.0), axis=0, keepdims=True)
            proj_ref[pl.ds(r, 1), :] = jnp.sum(jnp.where(drows == r, full[N:], 0.0), axis=0, keepdims=True)
        return 0

    lax.fori_loop(0, total // step, some, 0)
    out_ref[2 * total] = jnp.concatenate([diag_ref[...], proj_ref[...]], axis=0).astype(BF16)


def grams(obs_count, obs_anomaly, innovation, first, step=8):
    regions, slots, _ = obs_anomaly.shape
    hbm = pl.BlockSpec(memory_space=pltpu.HBM)
    return pl.pallas_call(
        functools.partial(gram_kernel, step, first),
        out_shape=jax.ShapeDtypeStruct((2 * CHUNK + 1, HALF // 2, N), BF16),
        in_specs=[hbm, hbm, hbm],
        out_specs=pl.BlockSpec(memory_space=pltpu.VMEM),
        scratch_shapes=[
            pltpu.SMEM((regions,), jnp.int32),
            pltpu.VMEM((CHUNK, slots, N), BF16),
            pltpu.VMEM((CHUNK, slots), BF16),
            pltpu.VMEM((CHUNK, N), F32),
            pltpu.VMEM((CHUNK, N), F32),
            pltpu.SemaphoreType.DMA((CHUNK,)),
            pltpu.SemaphoreType.DMA((2,)),
        ],
        compiler_params=pltpu.CompilerParams(vmem_limit_bytes=63 << 20),
        name="grams",
    )(obs_count, obs_anomaly, innovation)


def split(x):
    high = x.astype(BF16)
    return high, (x - high.astype(F32)).astype(BF16)


def expand(pair_packed, diags, mat_ref, row_a, row_b):
    la, lb = pair_packed
    i, j = iota((HALF, N), 0), iota((HALF, N), 1)
    turned = jnp.concatenate([la, lb], axis=0).T
    top, bottom = turned[:HALF], turned[HALF:]
    top_r, bottom_r = pltpu.roll(top, HALF, 1), pltpu.roll(bottom, HALF, 1)
    ridge = jnp.where(i == j, N - 1.0, 0.0)
    for row, lp, tt, tl, tr, dg in (
        (row_a, la, top, bottom, top_r, diags[0]), (row_b, lb, top_r, bottom_r, top, diags[1]),
    ):
        mat_ref[pl.ds(row, HALF), :] = jnp.where(i <= j, lp, tt) + ridge
        corner = jnp.where(i + HALF > j, pltpu.roll(lp, HALF, 1), tr)
        corner = jnp.where(i + HALF == j, dg + (N - 1.0), corner)
        mat_ref[pl.ds(row + HALF, HALF), :] = jnp.where(j < HALF, tl, corner)


def factor(mat_ref, small_ref, begin, regions, kb):
    sub = iota((BLK, regions), 0)
    x = []
    for i in range(BLK):
        row = mat_ref[pl.ds(begin * N + kb + i, regions, stride=N), :]
        x.append(row.T[kb:kb + BLK])
    lower = []
    for i in range(BLK):
        scale = lax.rsqrt(x[i][i:i + 1])
        r = jnp.where(sub == i, 1.0, x[i]) * scale
        for j in range(i + 1, BLK):
            x[j] = jnp.where(sub == i, 0.0, x[j]) - (x[i][j:j + 1] * scale) * r
        lower.append(jnp.where(sub <= i, r, 0.0))
        yield
    inverse = []
    for a in range(BLK):
        z = lower[a][a:a + 1] * lower[a]
        for i in range(a + 1, BLK):
            z = z + lower[i][a:a + 1] * lower[i]
        inverse.append(z)
        if a % 2:
            yield
    per = N // BLK
    lane = iota((regions, N), 1)
    for start, block in ((0, lower), (BLK, inverse)):
        for part in range(BLK // per):
            turned = jnp.concatenate(block[part * per:(part + 1) * per], axis=0).T
            yield
            for q in range(per):
                row = jnp.where((lane >= q * BLK) & (lane < (q + 1) * BLK), turned, 0.0)
                small_ref[pl.ds(begin * 2 * BLK + start + part * per + q, regions, stride=2 * BLK), :] = row


def products(mat_ref, small_ref, z_ref, begin, regions, kb):
    for m in range(begin, begin + regions):
        reduce_rows(mat_ref, small_ref, z_ref, m, kb)
        yield
    if kb + BLK < N:
        for m in range(begin, begin + regions):
            update(mat_ref, z_ref, m, kb)
            yield


def beside(one, other):
    live = [one, other]
    while live:
        for part in list(live):
            if next(part, live) is live:
                live.remove(part)


def reduce_rows(mat_ref, small_ref, z_ref, m, kb):
    start = m * N + kb
    rows = mat_ref[pl.ds(start, BLK), :]
    lane, sub = iota((BLK, N), 1), iota((BLK, N), 0)
    inside = (lane >= kb) & (lane < kb + BLK)
    rows = jnp.where(inside, jnp.where(lane - kb == sub, 1.0, 0.0), rows)
    rh, rl = split(rows)
    sh, sl = split(small_ref[pl.ds(m * 2 * BLK, 2 * BLK), :])
    both = mul_m(sh, sl, jnp.concatenate([rh] * (N // BLK), axis=0), jnp.concatenate([rl] * (N // BLK), axis=0))
    mat_ref[pl.ds(start, BLK), :] = jnp.where(lane < kb + BLK, both[:BLK], 0.0)
    z_ref[pl.ds(m * BLK, BLK), :] = both[BLK:]


def mul_k(ah, al, bh, bl):
    right = jnp.concatenate([
        jnp.concatenate([bh, bl], axis=1), jnp.concatenate([bh, jnp.zeros_like(bl)], axis=1)], axis=0)
    both = jnp.dot(jnp.concatenate([ah, al], axis=1), right, preferred_element_type=F32)
    return both[:, :N] + both[:, N:]


def mul_m(ah, al, bh, bl):
    n = ah.shape[0]
    both = jnp.dot(jnp.concatenate([ah, al], axis=0), jnp.concatenate([bh, bl], axis=1), preferred_element_type=F32)
    return (both[:n, :N] + both[:n, N:]) + both[n:, :N]


def update(mat_ref, z_ref, m, kb):
    n = N - kb - BLK
    start = m * N + kb + BLK
    mat = mat_ref[pl.ds(start, n), :]
    high, low = split(mat)
    zh, zl = split(z_ref[pl.ds(m * BLK, BLK), :])
    above, below = jnp.zeros((kb, N), BF16), jnp.zeros((n, N), BF16)

    def place(z):
        return jnp.concatenate([p for p in (above, z, below) if p.shape[0]], axis=0)

    change = mul_k(high, low, place(zh), place(zl))
    lane = iota((n, N), 1)
    kept = jnp.where((lane >= kb) & (lane < kb + BLK), 0.0, mat)
    mat_ref[pl.ds(start, n), :] = kept - change


def update_kernel(idx_ref, taper_ref, idxv_ref, taperv_ref, pmean_ref, param_ref, *rest):
    chunks = idxv_ref.shape[0] // CHUNK
    parts, rest = rest[:3 * chunks], rest[3 * chunks:]
    (out_ref, wide_ref, mat_ref, small_ref, z_ref, diag_ref, mean_ref, held_ref, made_ref,
     held_sem, made_sems) = rest
    regions, nb = idxv_ref.shape
    held = pltpu.make_async_copy(param_ref, held_ref, held_sem)
    held.start()
    for s, src in enumerate(parts):
        wide_ref[pl.ds(s * 2 * CHUNK, 2 * CHUNK)] = src[pl.ds(0, 2 * CHUNK)]
    tails = [src[2 * CHUNK].astype(F32) for src in parts]
    sel_lane = iota((regions, 3 * regions), 1)
    weights = jnp.zeros((regions, 3 * regions), F32)
    for k in range(nb):
        weights = weights + jnp.where(sel_lane == idxv_ref[:, k:k + 1], taperv_ref[:, k:k + 1], 0.0)
    diag_all = jnp.concatenate([t[:CHUNK] for t in tails], axis=0)
    proj_all = jnp.concatenate([t[CHUNK:] for t in tails], axis=0)
    diag_ref[...] = jnp.dot(weights, diag_all, precision=lax.Precision.HIGHEST, preferred_element_type=F32)
    proj = jnp.dot(weights, proj_all, precision=lax.Precision.HIGHEST, preferred_element_type=F32)

    def combine(pair, _):
        packed = []
        for q in range(2):
            r = 2 * pair + q
            acc = None
            for k in range(nb):
                tile = wide_ref[pl.ds(2 * idx_ref[r, k], 2)].reshape(HALF, N)
                term = taper_ref[r, k] * tile.astype(F32)
                acc = term if acc is None else acc + term
            packed.append(acc)
        row = pl.multiple_of(2 * pair * N, N)
        expand(packed, [diag_ref[pl.ds(2 * pair + q, 1), :] for q in range(2)], mat_ref, row, row + N)
        return 0

    lax.fori_loop(0, regions // 2, combine, 0, unroll=8)
    count = regions // 2
    before = iter(())
    for kb in range(0, N, BLK):
        for begin in (0, count):
            beside(factor(mat_ref, small_ref, begin, count, kb), before)
            before = products(mat_ref, small_ref, z_ref, begin, count, kb)
    for _ in before:
        pass

    def weigh(t, mean):
        for u in range(32):
            w = mat_ref[pl.ds(t * 32 + u, regions, stride=N), :]
            mean = mean + jnp.sum(w * proj, axis=1, keepdims=True) * w
        return mean

    mean_ref[...] = lax.fori_loop(0, N // 32, weigh, jnp.zeros((regions, N), F32))

    left_over = pmean_ref[...]
    pieces = []
    for _ in range(3):
        high = left_over.astype(BF16).astype(F32)
        pieces.append(high)
        left_over = left_over - high
    pieces.append(jnp.zeros((N - 3 * regions, left_over.shape[1]), F32))
    columns = jnp.concatenate(pieces, axis=0).T.astype(BF16)
    held.wait()

    def out_copy(m):
        return pltpu.make_async_copy(made_ref.at[m], out_ref.at[m], made_sems.at[m])

    def finish(t, _):
        lane = iota((N, N), 1)
        for u in range(U3):
            m = t * U3 + u
            w = mat_ref[pl.ds(pl.multiple_of(m * N, N), N), :]
            turned = (jnp.sqrt(jnp.float32(N - 1)) * w + mean_ref[pl.ds(m, 1), :]).astype(BF16)
            pick = ((lane == m) | (lane == regions + m) | (lane == 2 * regions + m)).astype(F32).astype(BF16)
            moved = lax.dot_general(
                jnp.concatenate([held_ref[m], columns], axis=1), jnp.concatenate([turned, pick], axis=1),
                (((1,), (1,)), ((), ())), preferred_element_type=F32,
            )
            made_ref[m] = moved.astype(BF16)
        for u in range(U3):
            out_copy(t * U3 + u).start()
        return 0

    lax.fori_loop(0, regions // U3, finish, 0)
    for m in range(regions):
        out_copy(m).wait()


def solve_update(idx, taper, parts, param_mean, param_anomaly):
    regions, nb = idx.shape
    hbm = pl.BlockSpec(memory_space=pl.ANY)
    smem = pl.BlockSpec(memory_space=pltpu.SMEM)
    vmem = pl.BlockSpec(memory_space=pltpu.VMEM)
    return pl.pallas_call(
        update_kernel,
        out_shape=jax.ShapeDtypeStruct(param_anomaly.shape, BF16),
        in_specs=[smem, smem, vmem, vmem, vmem, hbm] + [vmem] * len(parts),
        out_specs=hbm,
        scratch_shapes=[
            pltpu.VMEM((6 * regions, HALF // 2, N), BF16),
            pltpu.VMEM((regions * N, N), F32),
            pltpu.VMEM((regions * 2 * BLK, N), F32),
            pltpu.VMEM((regions * BLK, N), F32),
            pltpu.VMEM((regions, N), F32),
            pltpu.VMEM((regions, N), F32),
            pltpu.VMEM(param_anomaly.shape, BF16),
            pltpu.VMEM(param_anomaly.shape, BF16),
            pltpu.SemaphoreType.DMA,
            pltpu.SemaphoreType.DMA((regions,)),
        ],
        compiler_params=pltpu.CompilerParams(vmem_limit_bytes=50 << 20),
        name="solve_update",
    )(idx, taper, idx, taper, param_mean, param_anomaly, *parts)


def body(obs_anomaly, innovation, obs_count, neighbour, taper, param_anomaly, param_mean):
    regions = obs_anomaly.shape[0]
    size, half = lax.axis_size("region"), lax.axis_size("obs")
    total = regions * size
    here = lax.axis_index("region")
    devices = [(r, o) for r in range(size) for o in range(half)]

    def swap(x, other):
        line = [(r * half + o, (lambda a: (a[0] % size) * half + a[1])(other(r, o))) for r, o in devices]
        return lax.ppermute(x, ("region", "obs"), line)

    own, near, far = [], [], []
    for first in range(0, regions, CHUNK):
        packed = grams(obs_count, obs_anomaly, innovation, first)
        partner = swap(packed, lambda r, o: (r, 1 - o))
        both = (packed.astype(F32) + partner.astype(F32)).astype(BF16)
        own.append(both)
        far.append(swap(both, lambda r, o: (r + 1 if r % 2 else r - 1, 1 - o)))
        near.append(swap(both, lambda r, o: (r ^ 1, o)))
    place = (neighbour - here * regions + regions) % total
    even = here % 2 == 0
    before, after = jnp.where(even, 2, 1), jnp.where(even, 1, 2)
    slot = jnp.where(place < regions, before, jnp.where(place < 2 * regions, 0, after))
    idx = (slot * regions + place % regions).astype(jnp.int32)
    return solve_update(idx, taper, own + near + far, param_mean, param_anomaly)


def solution(mesh):
    specs = (
        P("region", "obs", None), P("region", "obs"), P("region"), P("region", None),
        P("region", None), P("region", "obs", None), P("region", "obs"),
    )
    return jax.shard_map(body, mesh=mesh, in_specs=specs, out_specs=P("region", "obs", None), check_vma=False)
```
